32 devices in a mesh: rep: 2 (over y), shard: 16 (over z, x, core).
Axes of the slice: x: 2, y: 2, z: 4, core: 2. Of those that a mesh axis runs over, the one named last changes fastest.
Arguments:
- tokens: bfloat16 [64, 256, 1152], P(('rep', 'shard')), may hold values from -6 to 6
- cotangent: bfloat16 [64, 256, 1152], P(('rep', 'shard')), may hold values from -6 to 6
- segments: int32 [64, 256], P(('rep', 'shard')), may hold values from 0 to 3, as said below
- norm_gains: float32 [4, 1152], replicated, may hold values from 0.5 to 1.5
- head_gains: float32 [2, 256], replicated, may hold values from 0.5 to 1.5
- qkv_weight: float32 [1152, 1536], P(None, 'shard'), may hold values from -0.1875 to 0.1875
- out_weight: float32 [1024, 1152], P('shard'), may hold values from -0.1875 to 0.1875
- gate_up_weight: float32 [1152, 13824], P(None, 'shard'), may hold values from -0.1875 to 0.1875
- down_weight: float32 [6912, 1152], P('shard'), may hold values from -0.078125 to 0.078125
- qkv_left: float32 [32, 9, 128, 128], P('shard'), as said below
- qkv_right: float32 [32, 9, 48, 48], P('shard'), as said below
- qkv_left_root: float32 [32, 9, 128, 128], P('shard'), as said below
- qkv_right_root: float32 [32, 9, 48, 48], P('shard'), as said below
- out_left: float32 [32, 9, 32, 32], P('shard'), as said below
- out_right: float32 [32, 9, 128, 128], P('shard'), as said below
- out_left_root: float32 [32, 9, 32, 32], P('shard'), as said below
- out_right_root: float32 [32, 9, 128, 128], P('shard'), as said below
- gate_up_left: float32 [32, 9, 128, 128], P('shard'), as said below
- gate_up_right: float32 [32, 9, 432, 432], P('shard'), as said below
- gate_up_left_root: float32 [32, 9, 128, 128], P('shard'), as said below
- gate_up_right_root: float32 [32, 9, 432, 432], P('shard'), as said below
- down_left: float32 [32, 9, 216, 216], P('shard'), as said below
- down_right: float32 [32, 9, 128, 128], P('shard'), as said below
- down_left_root: float32 [32, 9, 216, 216], P('shard'), as said below
- down_right_root: float32 [32, 9, 128, 128], P('shard'), as said below
- decay: float32 [4], replicated, may hold values from 0.4 to 0.6
- rate: float32 [4], replicated, may hold values from 0.02 to 0.2
Outputs:
- block_output: bfloat16 [64, 256, 1152], P(('rep', 'shard'))
- input_grad: float32 [64, 256, 1152], P(('rep', 'shard'))
- norm_gain_grad: float32 [4, 1152], P(None, 'shard')
- head_gain_grad: float32 [2, 256], P(None, 'shard')
- qkv_grad: float32 [1152, 1536], P(None, 'shard')
- out_grad: float32 [1024, 1152], P('shard')
- gate_up_grad: float32 [1152, 13824], P(None, 'shard')
- down_grad: float32 [6912, 1152], P('shard')
- qkv_new: float32 [1152, 1536], P(None, 'shard')
- out_new: float32 [1024, 1152], P('shard')
- gate_up_new: float32 [1152, 13824], P(None, 'shard')
- down_new: float32 [6912, 1152], P('shard')
- qkv_left_new: float32 [32, 9, 128, 128], P('shard')
- qkv_right_new: float32 [32, 9, 48, 48], P('shard')
- out_left_new: float32 [32, 9, 32, 32], P('shard')
- out_right_new: float32 [32, 9, 128, 128], P('shard')
- gate_up_left_new: float32 [32, 9, 128, 128], P('shard')
- gate_up_right_new: float32 [32, 9, 432, 432], P('shard')
- down_left_new: float32 [32, 9, 216, 216], P('shard')
- down_right_new: float32 [32, 9, 128, 128], P('shard')
The draws below stay inside these ranges and needn't reach their ends.
Inputs may be any that keep to these rules, and one draw needn't show every extreme that they name: `segments`: in each group the prompt (segment 0) comes first with 64 to 128 tokens, then continuations 1 to 3 in order, each of 16 tokens or more. `qkv_left`: each block is symmetric positive definite. `qkv_right`: each block is symmetric positive definite. `qkv_left_root`: each block is symmetric positive definite. `qkv_right_root`: each block is symmetric positive definite. `out_left`: each block is symmetric positive definite. `out_right`: each block is symmetric positive definite. `out_left_root`: each block is symmetric positive definite. `out_right_root`: each block is symmetric positive definite. `gate_up_left`: each block is symmetric positive definite. `gate_up_right`: each block is symmetric positive definite. `gate_up_left_root`: each block is symmetric positive definite. `gate_up_right_root`: each block is symmetric positive definite. `down_left`: each block is symmetric positive definite. `down_right`: each block is symmetric positive definite. `down_left_root`: each block is symmetric positive definite. `down_right_root`: each block is symmetric positive definite.
All inputs are finite; a program needn't handle non-finite values.
Results may differ from the reference program's by a relative error of at most 0.024.
Values may be sent and summed in bfloat16 or wider, within the bound.
A program may use at most 384 MiB of HBM per device.

```python
import math
import jax
import jax.numpy as jnp
from jax import lax

D = 1152
HQ = 4
HD = 256
FF = 6912
RB = 128
STRIPS = 32
CONT = 3
GLEN = 256
QKV = 1536
DB = 9
QB = 48
OB = 32
GB = 432
FB = 216
GROUPS = 64
TOKENS = 16384


def spd_blocks(key, tag, size, scale):
    own_key = jax.random.fold_in(key, tag)
    first_key, second_key = jax.random.split(own_key)
    noise = jax.random.uniform(first_key, (STRIPS, DB, size, size), jnp.float32, -1.0, 1.0)
    mirrored = (noise + jnp.swapaxes(noise, -1, -2)) * (0.5 * 0.95 / size)
    diagonal = jax.random.uniform(second_key, (STRIPS, DB, size), jnp.float32, 1.0, 2.0)
    identity = jnp.eye(size, dtype=jnp.float32)
    return scale * (mirrored * (1.0 - identity) + identity * diagonal[..., None])


def draw_segments(key, part):
    keys_all = jax.random.split(key, CONT + 1)
    least = max(GLEN // 16, 1)
    prompt = jax.random.randint(keys_all[0], (GROUPS,), GLEN // 4, GLEN // 2 + 1)
    places = jnp.arange(GLEN, dtype=jnp.int32)[None, :]
    bounds = prompt
    labels = (places >= bounds[:, None]).astype(jnp.int32)
    remaining = GLEN - prompt
    for turn in range(CONT - 1):
        after = CONT - 1 - turn
        length = jax.random.randint(keys_all[turn + 1], (GROUPS,), least, remaining - after * least + 1)
        bounds = bounds + length
        labels = labels + (places >= bounds[:, None]).astype(jnp.int32)
        remaining = remaining - length
    return labels


def draw_qkv_left(key, part):
    return spd_blocks(key, 101, RB, 2.0 * QB)


def draw_qkv_right(key, part):
    return spd_blocks(key, 102, QB, 2.0 * RB)


def draw_qkv_left_root(key, part):
    return spd_blocks(key, 103, RB, (0.25 * QB) ** (-0.25))


def draw_qkv_right_root(key, part):
    return spd_blocks(key, 104, QB, (0.25 * RB) ** (-0.25))


def draw_out_left(key, part):
    return spd_blocks(key, 105, OB, 2.0 * RB)


def draw_out_right(key, part):
    return spd_blocks(key, 106, RB, 2.0 * OB)


def draw_out_left_root(key, part):
    return spd_blocks(key, 107, OB, (0.25 * RB) ** (-0.25))


def draw_out_right_root(key, part):
    return spd_blocks(key, 108, RB, (0.25 * OB) ** (-0.25))


def draw_gate_up_left(key, part):
    return spd_blocks(key, 109, RB, 0.25 * GB)


def draw_gate_up_right(key, part):
    return spd_blocks(key, 110, GB, 0.25 * RB)


def draw_gate_up_left_root(key, part):
    return spd_blocks(key, 111, RB, (0.25 * GB) ** (-0.25))


def draw_gate_up_right_root(key, part):
    return spd_blocks(key, 112, GB, (0.25 * RB) ** (-0.25))


def draw_down_left(key, part):
    return spd_blocks(key, 113, FB, 0.25 * RB)


def draw_down_right(key, part):
    return spd_blocks(key, 114, RB, 2.0 * FB)


def draw_down_left_root(key, part):
    return spd_blocks(key, 115, FB, (0.25 * RB) ** (-0.25))


def draw_down_right_root(key, part):
    return spd_blocks(key, 116, RB, (0.25 * FB) ** (-0.25))


def shard_levels(stream_key, dims, pieces, low, high):
    loudness = 1.0
    for axis_at, shards_of in pieces:
        draws = jax.random.uniform(jax.random.fold_in(jax.random.fold_in(stream_key, 6), axis_at), (shards_of,), jnp.float32, low / len(pieces), high / len(pieces))
        loudness = loudness * jnp.repeat(jnp.exp(draws), dims[axis_at] // shards_of).reshape((-1,) + (1,) * (len(dims) - 1 - axis_at))
    return loudness


def centred(key, dims, deviation, reach, pieces=(), kind=jnp.bfloat16):
    drawn = jax.random.normal(key, dims, jnp.float32) * deviation
    if len(pieces) > 0:
        drawn = shard_levels(key, dims, pieces, -0.22, 0.18) * drawn
    return jnp.clip(drawn, min=-reach, max=reach).astype(kind)


def setup_inputs(seed: int = 0) -> dict:
    arg_keys = jax.random.split(jax.random.key(seed), 28)
    tokens = centred(arg_keys[0], (GROUPS, GLEN, D), 1.0, 6.0, ((0, 32),))
    cotangent = centred(arg_keys[1], (GROUPS, GLEN, D), 1.0, 6.0, ((0, 32),))
    segments = draw_segments(jax.random.fold_in(arg_keys[27], 71), 0)
    norm_gains = jnp.clip(1.0 + 0.1 * jax.random.normal(arg_keys[3], (4, D), jnp.float32), 0.5, 1.5)
    head_gains = jnp.clip(1.0 + 0.1 * jax.random.normal(arg_keys[4], (2, HD), jnp.float32), 0.5, 1.5)
    qkv_weight = centred(arg_keys[5], (D, QKV), D ** -0.5, 0.1875, ((1, 16),), jnp.float32)
    out_weight = centred(arg_keys[6], (HQ * HD, D), (HQ * HD) ** -0.5, 0.1875, ((0, 16),), jnp.float32)
    gate_up_weight = centred(arg_keys[7], (D, 2 * FF), D ** -0.5, 0.1875, ((1, 16),), jnp.float32)
    down_weight = centred(arg_keys[8], (FF, D), FF ** -0.5, 0.078125, ((0, 16),), jnp.float32)
    qkv_left = draw_qkv_left(jax.random.fold_in(arg_keys[27], 71), 0)
    qkv_right = draw_qkv_right(jax.random.fold_in(arg_keys[27], 71), 0)
    qkv_left_root = draw_qkv_left_root(jax.random.fold_in(arg_keys[27], 71), 0)
    qkv_right_root = draw_qkv_right_root(jax.random.fold_in(arg_keys[27], 71), 0)
    out_left = draw_out_left(jax.random.fold_in(arg_keys[27], 71), 0)
    out_right = draw_out_right(jax.random.fold_in(arg_keys[27], 71), 0)
    out_left_root = draw_out_left_root(jax.random.fold_in(arg_keys[27], 71), 0)
    out_right_root = draw_out_right_root(jax.random.fold_in(arg_keys[27], 71), 0)
    gate_up_left = draw_gate_up_left(jax.random.fold_in(arg_keys[27], 71), 0)
    gate_up_right = draw_gate_up_right(jax.random.fold_in(arg_keys[27], 71), 0)
    gate_up_left_root = draw_gate_up_left_root(jax.random.fold_in(arg_keys[27], 71), 0)
    gate_up_right_root = draw_gate_up_right_root(jax.random.fold_in(arg_keys[27], 71), 0)
    down_left = draw_down_left(jax.random.fold_in(arg_keys[27], 71), 0)
    down_right = draw_down_right(jax.random.fold_in(arg_keys[27], 71), 0)
    down_left_root = draw_down_left_root(jax.random.fold_in(arg_keys[27], 71), 0)
    down_right_root = draw_down_right_root(jax.random.fold_in(arg_keys[27], 71), 0)
    decay = jnp.clip(jax.random.uniform(arg_keys[25], (4,), jnp.float32, 0.4, 0.6), 0.4, 0.6)
    rate = jnp.clip(jnp.exp(jax.random.uniform(arg_keys[26], (4,), jnp.float32, math.log(0.02), math.log(0.2))), 0.02, 0.2)
    return dict(tokens=tokens, cotangent=cotangent, segments=segments, norm_gains=norm_gains, head_gains=head_gains, qkv_weight=qkv_weight, out_weight=out_weight, gate_up_weight=gate_up_weight, down_weight=down_weight, qkv_left=qkv_left, qkv_right=qkv_right, qkv_left_root=qkv_left_root, qkv_right_root=qkv_right_root, out_left=out_left, out_right=out_right, out_left_root=out_left_root, out_right_root=out_right_root, gate_up_left=gate_up_left, gate_up_right=gate_up_right, gate_up_left_root=gate_up_left_root, gate_up_right_root=gate_up_right_root, down_left=down_left, down_right=down_right, down_left_root=down_left_root, down_right_root=down_right_root, decay=decay, rate=rate)


@jax.custom_vjp
def low(v):
    return lax.optimization_barrier(v.astype(jnp.bfloat16)).astype(jnp.float32)

@jax.custom_vjp
def low_back(v):
    return v

def low_keep(v):
    return (low(v), None)

def low_pass(kept, grad):
    return (grad,)

def back_keep(v):
    return (v, None)

def back_low(kept, grad):
    return (low(grad),)
low.defvjp(low_keep, low_pass)
low_back.defvjp(back_keep, back_low)
epsilon = 1e-06
rope_base = 1000000.0
highest = lax.Precision.HIGHEST

def rms_norm(values, gains):
    return values * lax.rsqrt(lax.optimization_barrier(jnp.mean(values * values, axis=-1, keepdims=True)) + epsilon) * gains

def matmul(left_op, right_op):
    return jnp.dot(left_op, right_op, precision=highest, preferred_element_type=jnp.float32)

def positions(segment_ids):
    length = segment_ids.shape[0]
    places = jnp.arange(length, dtype=jnp.int32)
    prompt = jnp.sum((segment_ids == 0).astype(jnp.int32))
    before = lax.optimization_barrier(jnp.sum((segment_ids[None, :] < segment_ids[:, None]).astype(jnp.int32), axis=1))
    return jnp.where(segment_ids == 0, places, prompt + places - before)

def rope_tables(segment_ids):
    half = HD // 2
    spots = positions(segment_ids).astype(jnp.float32)
    freqs = jnp.exp(jnp.arange(half, dtype=jnp.float32) * (-2.0 * math.log(rope_base) / HD))
    angles = spots[:, None] * freqs[None, :]
    return (jnp.cos(angles), jnp.sin(angles))

def rotate(values, cosine, sine_part):
    half = values.shape[-1] // 2
    former = values[..., :half]
    latter = values[..., half:]
    return jnp.concatenate([former * cosine - latter * sine_part, latter * cosine + former * sine_part], axis=-1)

def allowed_pairs(segment_ids):
    length = segment_ids.shape[0]
    places = jnp.arange(length, dtype=jnp.int32)
    causal = places[:, None] >= places[None, :]
    shared = (segment_ids[None, :] == 0) | (segment_ids[None, :] == segment_ids[:, None])
    return causal & shared

def split_heads(qkv, head_gains, cosine, sine_part):
    length = qkv.shape[0]
    query_rows = qkv[:, :HQ * HD].reshape(length, HQ, HD)
    key_rows = qkv[:, HQ * HD:(HQ + 1) * HD]
    value_rows = qkv[:, (HQ + 1) * HD:]
    query_rows = rotate(rms_norm(query_rows, head_gains[0]), cosine[:, None, :], sine_part[:, None, :]) * HD ** (-0.5)
    key_rows = rotate(rms_norm(key_rows, head_gains[1]), cosine, sine_part)
    return (query_rows, key_rows, value_rows)

def geglu(gate_up):
    return jax.nn.gelu(gate_up[:, :FF], approximate=True) * gate_up[:, FF:]

def group_forward(block_in, segment_ids, params):
    norm_gains, head_gains, qkv_weight, out_weight, gate_up_weight, down_weight = params
    length = block_in.shape[0]
    cosine, sine_part = rope_tables(segment_ids)
    normed = low(rms_norm(block_in, norm_gains[0]))
    qkv = low_back(matmul(normed, low(qkv_weight)))
    query_rows, key_rows, value_rows = split_heads(qkv, head_gains, cosine, sine_part)
    query_rows = low(query_rows)
    key_rows = low(key_rows)
    value_rows = low(value_rows)
    scores = low_back(jnp.einsum('thd,sd->hts', query_rows, key_rows, precision=highest))
    scores = jnp.where(allowed_pairs(segment_ids)[None], scores, -1000000000.0)
    top_score = lax.optimization_barrier(jnp.max(scores, axis=-1, keepdims=True))
    exponent = jnp.exp(scores - top_score)
    attn_probs = exponent / lax.optimization_barrier(jnp.sum(exponent, axis=-1, keepdims=True))
    context = jnp.einsum('hts,sd->thd', low(attn_probs), value_rows, precision=highest).reshape(length, HQ * HD)
    context = low(low_back(context))
    attn_out = low_back(matmul(context, low(out_weight)))
    middle = block_in + rms_norm(attn_out, norm_gains[1])
    normed_ffn = low(rms_norm(middle, norm_gains[2]))
    gate_up = low_back(matmul(normed_ffn, low(gate_up_weight)))
    hidden = low(low_back(geglu(gate_up)))
    ffn_out = low_back(matmul(hidden, low(down_weight)))
    return middle + rms_norm(ffn_out, norm_gains[3])

def all_forward(block_in, segment_ids, params):
    per_round = math.gcd(GROUPS, max(1, 4096 // GLEN))
    rounds = GROUPS // per_round
    inputs = (block_in.reshape(rounds, per_round, GLEN, D), segment_ids.reshape(rounds, per_round, GLEN))

    def one_round(pair):
        return jax.vmap(lambda rows, ids: group_forward(rows, ids, params))(pair[0], pair[1])
    results = lax.map(jax.checkpoint(one_round), inputs)
    return results.reshape(GROUPS, GLEN, D)

def column_blocks(full, row_size, col_size):
    row_total, col_total = full.shape
    return full.reshape(row_total // row_size, row_size, col_total // col_size, col_size).transpose(2, 0, 1, 3)

def column_full(blocks):
    strip_count, row_count, row_size, col_size = blocks.shape
    return blocks.transpose(1, 2, 0, 3).reshape(row_count * row_size, strip_count * col_size)

def row_blocks(full, row_size, col_size):
    row_total, col_total = full.shape
    return full.reshape(row_total // row_size, row_size, col_total // col_size, col_size).transpose(0, 2, 1, 3)

def row_full(blocks):
    strip_count, col_count, row_size, col_size = blocks.shape
    return blocks.transpose(0, 2, 1, 3).reshape(strip_count * row_size, col_count * col_size)

def refresh(grad_blocks, weight_blocks, left_stat, right_stat, left_root, right_root, decay_rate, step_rate):
    new_left = decay_rate * left_stat + (1.0 - decay_rate) * jnp.einsum('sbij,sbkj->sbik', grad_blocks, grad_blocks, precision=highest)
    new_right = decay_rate * right_stat + (1.0 - decay_rate) * jnp.einsum('sbji,sbjk->sbik', grad_blocks, grad_blocks, precision=highest)
    step = jnp.einsum('sbij,sbjk->sbik', jnp.einsum('sbij,sbjk->sbik', left_root, grad_blocks, precision=highest), right_root, precision=highest)
    return (weight_blocks - step_rate * step, new_left, new_right)

def reference(tokens, cotangent, segments, norm_gains, head_gains, qkv_weight, out_weight, gate_up_weight, down_weight, qkv_left, qkv_right, qkv_left_root, qkv_right_root, out_left, out_right, out_left_root, out_right_root, gate_up_left, gate_up_right, gate_up_left_root, gate_up_right_root, down_left, down_right, down_left_root, down_right_root, decay, rate):
    block_in = tokens.astype(jnp.float32)
    params = (norm_gains, head_gains, qkv_weight, out_weight, gate_up_weight, down_weight)
    result, pull = jax.vjp(lambda rows, weights: all_forward(rows, segments, weights), block_in, params)
    input_grad, grads = pull(cotangent.astype(jnp.float32))
    norm_gain_grad, head_gain_grad, qkv_grad, out_grad, gate_up_grad, down_grad = grads
    scale = float(TOKENS) ** (-0.5)
    qkv_blocks, qkv_left_new, qkv_right_new = refresh(column_blocks(qkv_grad * scale, RB, QB), column_blocks(qkv_weight, RB, QB), qkv_left, qkv_right, qkv_left_root, qkv_right_root, decay[0], rate[0])
    out_blocks, out_left_new, out_right_new = refresh(row_blocks(out_grad * scale, OB, RB), row_blocks(out_weight, OB, RB), out_left, out_right, out_left_root, out_right_root, decay[1], rate[1])
    gate_up_blocks, gate_up_left_new, gate_up_right_new = refresh(column_blocks(gate_up_grad * scale, RB, GB), column_blocks(gate_up_weight, RB, GB), gate_up_left, gate_up_right, gate_up_left_root, gate_up_right_root, decay[2], rate[2])
    down_blocks, down_left_new, down_right_new = refresh(row_blocks(down_grad * scale, FB, RB), row_blocks(down_weight, FB, RB), down_left, down_right, down_left_root, down_right_root, decay[3], rate[3])
    return (result.astype(jnp.bfloat16), input_grad, norm_gain_grad, head_gain_grad, qkv_grad, out_grad, gate_up_grad, down_grad, column_full(qkv_blocks), row_full(out_blocks), column_full(gate_up_blocks), row_full(down_blocks), qkv_left_new, qkv_right_new, out_left_new, out_right_new, gate_up_left_new, gate_up_right_new, down_left_new, down_right_new)
```

```python
import math

import jax
import jax.numpy as jnp
from jax import lax
from jax.sharding import PartitionSpec as P

HQ = 4
HD = 256
AXES = ("rep", "shard")
PAD = 16

epsilon = 1e-06
rope_base = 1000000.0
low = jnp.bfloat16
full = jnp.float32


def dot(a, b, ca, cb):
    return lax.dot_general(a, b, (((ca,), (cb,)), ((), ())), preferred_element_type=full)


class Place:
    def __init__(self, mesh):
        self.reps = mesh.shape["rep"]
        self.shards = mesh.shape["shard"]
        self.chips = self.shards // 2
        self.outer = min(4, self.chips)
        self.inner = self.chips // self.outer

    def here(self):
        r, i = lax.axis_index("rep"), lax.axis_index("shard")
        chip = i // 2
        return r % 2, chip // self.inner, chip % self.inner, i % 2

    def send(self, value, where):
        pairs = []
        for r in range(self.reps):
            for i in range(self.shards):
                o, n, c = i // 2 // self.inner, i // 2 % self.inner, i % 2
                to = where(r, o, n, c)
                if to is not None:
                    r2, o2, n2, c2 = to
                    pairs.append((r * self.shards + i, r2 * self.shards + (o2 * self.inner + n2) * 2 + c2))
        return lax.ppermute(value, AXES, pairs)

    def swap_rep(self, value):
        return self.send(value, lambda r, o, n, c: (r ^ 1, o, n, c))

    def swap_core(self, value):
        return self.send(value, lambda r, o, n, c: (r, o, n, 1 - c))

    def line(self, value, size, move, index):
        up, down = [], []
        send_up = send_down = value
        for k in range(size - 1):
            send_up = move(send_up, 1)
            send_down = move(send_down, -1)
            up.append(send_up)
            down.append(send_down)
        window = jnp.stack(up[::-1] + [value] + down)
        return lax.dynamic_slice_in_dim(window, size - 1 - index, size, 0)

    def move_outer(self, value, by, keep=None):
        def where(r, o, n, c):
            if keep is not None and not keep(n, c):
                return None
            return (r, o + by, n, c) if 0 <= o + by < self.outer else None

        return self.send(value, where)

    def move_inner(self, value, by, keep=None):
        def where(r, o, n, c):
            if keep is not None and not keep(n, c):
                return None
            return (r, o, n + by, c) if 0 <= n + by < self.inner else None

        return self.send(value, where)

    def gather_outer(self, value, keep=None):
        o = self.here()[1]
        return self.line(value, self.outer, lambda v, by: self.move_outer(v, by, keep), o)

    def gather_chips(self, value):
        n = self.here()[2]
        columns = self.gather_outer(value)
        if self.inner == 2:
            other = self.send(columns, lambda r, o, n, c: (r, o, 1 - n, c))
            both = jnp.where(n == 0, jnp.stack([columns, other], 1), jnp.stack([other, columns], 1))
        else:
            both = jnp.swapaxes(self.line(columns, self.inner, self.move_inner, n), 0, 1)
        return both.reshape((self.chips,) + value.shape)

    def scatter_line(self, parts, size, move, index):
        zeros = jnp.zeros_like(parts[:1])
        padded = jnp.concatenate([zeros] * (size - 1) + [parts] + [zeros] * (size - 1), 0)

        def part(offset):
            return lax.dynamic_index_in_dim(padded, index + offset + size - 1, 0, keepdims=False)

        sums = []
        for way in (1, -1):
            got = None
            for k in range(size - 1, 0, -1):
                mine = part(way * k)
                if got is not None:
                    mine = (mine.astype(full) + got.astype(full)).astype(low)
                got = move(mine, way)
            sums.append(got)
        return (part(0).astype(full) + sums[0].astype(full) + sums[1].astype(full)).astype(low)

    def scatter_outer(self, parts, keep=None):
        o = self.here()[1]
        return self.scatter_line(parts, self.outer, lambda v, by: self.move_outer(v, by, keep), o)

    def scatter_chips(self, parts):
        n = self.here()[2]
        parts = parts.reshape((self.outer, self.inner) + parts.shape[1:])
        if self.inner == 2:
            away = lax.dynamic_index_in_dim(parts, 1 - n, 1, keepdims=False)
            mine = lax.dynamic_index_in_dim(parts, n, 1, keepdims=False)
            got = self.send(away, lambda r, o, n, c: (r, o, 1 - n, c))
            column = (mine.astype(full) + got.astype(full)).astype(low)
        else:
            column = self.scatter_line(jnp.swapaxes(parts, 0, 1), self.inner, self.move_inner, n)
        return self.scatter_outer(column)

    def gather_down(self, block):
        par, o, n, c = self.here()
        other = self.swap_core(block)
        mine = jnp.where(par == c, block, other)
        if self.inner == 2:
            keep = lambda n, c: n == c
            column = self.gather_outer(mine, keep)
            got = self.send(column, lambda r, o, n, c: (r, o, 1 - n, c) if n == c else None)
            return jnp.where(n == c, column, got)
        both = self.gather_chips(mine)
        both = both.reshape((self.chips // 2, 2) + block.shape)
        return lax.dynamic_index_in_dim(both, c, 1, keepdims=False)

    def scatter_down(self, parts):
        par, o, n, c = self.here()
        if self.inner == 2:
            keep = lambda n, c: n == c
            got = self.send(parts, lambda r, o, n, c: (r, o, 1 - n, c) if n != c else None)
            column = (parts.astype(full) + got.astype(full)).astype(low)
            own = self.scatter_outer(column, keep)
        else:
            zeros = jnp.zeros_like(parts)
            both = jnp.where(c == 0, jnp.stack([parts, zeros], 1), jnp.stack([zeros, parts], 1))
            own = self.scatter_chips(both.reshape((self.chips,) + parts.shape[1:]))
        own = self.sum_pairs(own)
        far = self.send(own, lambda r, o, n, c: (r ^ 1, o, n, r % 2) if c == n % 2 else None)
        near = self.send(own, lambda r, o, n, c: (r, o, n, r % 2) if c == n % 2 and c != r % 2 else None)
        return jnp.where(c != par, far, jnp.where(c == n % 2, own, near))

    def sum_pairs(self, value):
        if self.reps == 2:
            return value
        groups = [list(range(k, self.reps, 2)) for k in range(2)]
        return lax.psum(value, "rep", axis_index_groups=groups)

    def gather_tokens(self, rows):
        two = jnp.concatenate([rows, self.swap_rep(rows)], 0)
        return jnp.concatenate([two, self.swap_core(two)], 0)

    def scatter_tokens(self, rows):
        half, quarter = rows.shape[0] // 2, rows.shape[0] // 4
        two = rows[:half] + self.swap_core(rows[half:].astype(low)).astype(full)
        return two[:quarter] + self.swap_rep(two[quarter:].astype(low)).astype(full)


def rms_norm(values, gains):
    return values * lax.rsqrt(jnp.mean(values * values, axis=-1, keepdims=True) + epsilon) * gains


def positions(segment_ids):
    length = segment_ids.shape[0]
    places = jnp.arange(length, dtype=jnp.int32)
    prompt = jnp.sum((segment_ids == 0).astype(jnp.int32))
    before = jnp.sum((segment_ids[None, :] < segment_ids[:, None]).astype(jnp.int32), axis=1)
    return jnp.where(segment_ids == 0, places, prompt + places - before)


def rope_tables(segment_ids):
    half = HD // 2
    spots = positions(segment_ids).astype(full)
    freqs = jnp.exp(jnp.arange(half, dtype=full) * (-2.0 * math.log(rope_base) / HD))
    angles = spots[:, None] * freqs[None, :]
    return (jnp.cos(angles), jnp.sin(angles))


def rotate(values, cosine, sine_part):
    half = values.shape[-1] // 2
    former = values[..., :half]
    latter = values[..., half:]
    return jnp.concatenate(
        [former * cosine - latter * sine_part, latter * cosine + former * sine_part], axis=-1
    )


def allowed_pairs(segment_ids):
    length = segment_ids.shape[0]
    places = jnp.arange(length, dtype=jnp.int32)
    causal = places[:, None] >= places[None, :]
    shared = (segment_ids[None, :] == 0) | (segment_ids[None, :] == segment_ids[:, None])
    return causal & shared


def split_heads(qkv, head_gains, cosine, sine_part):
    length = qkv.shape[0]
    query_rows = qkv[:, : HQ * HD].reshape(length, HQ, HD)
    key_rows = qkv[:, HQ * HD : (HQ + 1) * HD]
    value_rows = qkv[:, (HQ + 1) * HD :]
    query_rows = rotate(
        rms_norm(query_rows, head_gains[0]), cosine[:, None, :], sine_part[:, None, :]
    ) * HD ** (-0.5)
    key_rows = rotate(rms_norm(key_rows, head_gains[1]), cosine, sine_part)
    return (query_rows, key_rows, value_rows)


def attend(query_low, key_low, value_low, allowed):
    scores = jnp.einsum("thd,sd->hts", query_low, key_low, preferred_element_type=full)
    scores = jnp.where(allowed[None], scores, -1000000000.0)
    exponent = jnp.exp(scores - jnp.max(scores, axis=-1, keepdims=True))
    probs = exponent / jnp.sum(exponent, axis=-1, keepdims=True)
    context = jnp.einsum("hts,sd->thd", probs.astype(low), value_low, preferred_element_type=full)
    return probs, context.reshape(context.shape[0], HQ * HD).astype(low)


def attend_back(context_grad, probs, query_low, key_low, value_low):
    context_grad = context_grad.reshape(context_grad.shape[0], HQ, HD)
    prob_grad = jnp.einsum("thd,sd->hts", context_grad, value_low, preferred_element_type=full)
    row_dot = jnp.sum(prob_grad * probs, axis=-1, keepdims=True)
    score_grad = (probs * (prob_grad - row_dot)).astype(low)
    query_grad = jnp.einsum("hts,sd->thd", score_grad, key_low, preferred_element_type=full)
    key_grad = jnp.einsum("hts,thd->sd", score_grad, query_low, preferred_element_type=full)
    value_grad = jnp.einsum("hts,thd->sd", probs.astype(low), context_grad, preferred_element_type=full)
    return query_grad, key_grad, value_grad


def gelu_parts(gate):
    c = math.sqrt(2.0 / math.pi)
    t = jnp.tanh(c * (gate + 0.044715 * gate * gate * gate))
    cdf = 0.5 * (1.0 + t)
    slope = cdf + 0.5 * gate * (1.0 - t * t) * (c * (1.0 + 3.0 * 0.044715 * gate * gate))
    return gate * cdf, slope


def column_blocks(whole, row_size, col_size):
    rows, cols = whole.shape
    return whole.reshape(rows // row_size, row_size, cols // col_size, col_size).transpose(2, 0, 1, 3)


def column_full(blocks):
    strips, count, row_size, col_size = blocks.shape
    return blocks.transpose(1, 2, 0, 3).reshape(count * row_size, strips * col_size)


def row_blocks(whole, row_size, col_size):
    rows, cols = whole.shape
    return whole.reshape(rows // row_size, row_size, cols // col_size, col_size).transpose(0, 2, 1, 3)


def row_full(blocks):
    strips, count, row_size, col_size = blocks.shape
    return blocks.transpose(0, 2, 1, 3).reshape(strips * row_size, count * col_size)


def refresh(grads, weights, left_stat, right_stat, left_root, right_root, decay_rate, step_rate):
    def mul(spec, a, b):
        return jnp.einsum(spec, a.astype(low), b.astype(low), preferred_element_type=full)

    new_left = decay_rate * left_stat + (1.0 - decay_rate) * mul("sbij,sbkj->sbik", grads, grads)
    new_right = decay_rate * right_stat + (1.0 - decay_rate) * mul("sbji,sbjk->sbik", grads, grads)
    step = mul("sbij,sbjk->sbik", mul("sbij,sbjk->sbik", left_root, grads), right_root)
    return (weights - step_rate * step, new_left, new_right)


def per_device(place, tokens, cotangent, segments, norm_gains, head_gains, *rest):
    qkv_weight, out_weight, gate_up_weight, down_weight = rest[:4]
    stats = rest[4:20]
    decay, rate = rest[20:]
    groups, length, width = tokens.shape
    par, outer, inner, core = place.here()
    qw, ow = qkv_weight.shape[1], out_weight.shape[0]
    unit = down_weight.shape[0]

    attn_own = jnp.concatenate([qkv_weight.T, out_weight], 0).astype(low)
    both = place.gather_chips(attn_own)
    mate = place.swap_core(both)
    both = jnp.where(core == 0, jnp.stack([both, mate], 1), jnp.stack([mate, both], 1))
    qkv_mat = both[:, :, :qw].reshape(place.shards * qw, width)
    out_mat = both[:, :, qw:].reshape(place.shards * ow, width)
    gate_up_own = lax.dynamic_index_in_dim(
        gate_up_weight.T.astype(low).reshape(2, unit, width), par, 0, keepdims=False
    )
    gate_up_all = place.gather_chips(gate_up_own)
    hidden_count = place.chips // 2 * unit
    gate_mat = gate_up_all[: place.chips // 2].reshape(hidden_count, width)
    up_mat = gate_up_all[place.chips // 2 :].reshape(hidden_count, width)
    down_mat = place.gather_down(down_weight.astype(low)).reshape(hidden_count, width)

    block_in = tokens.astype(full).reshape(groups * length, width)
    cosine, sine_part = jax.vmap(rope_tables)(segments)
    allowed = jax.vmap(allowed_pairs)(segments)
    normed = rms_norm(block_in, norm_gains[0]).astype(low)
    qkv = dot(normed, qkv_mat, 1, 1).reshape(groups, length, -1)
    query_rows, key_rows, value_rows = jax.vmap(split_heads, (0, None, 0, 0))(
        qkv, head_gains, cosine, sine_part
    )
    query_low, key_low, value_low = query_rows.astype(low), key_rows.astype(low), value_rows.astype(low)
    probs, context = jax.vmap(attend)(query_low, key_low, value_low, allowed)
    context = context.reshape(groups * length, HQ * HD)
    attn_out = dot(context, out_mat, 1, 0)
    middle = block_in + rms_norm(attn_out, norm_gains[1])
    normed_ffn = rms_norm(middle, norm_gains[2]).astype(low)
    normed_all = place.gather_tokens(normed_ffn)
    gate = dot(normed_all, gate_mat, 1, 1)
    up = dot(normed_all, up_mat, 1, 1)
    act, slope = gelu_parts(gate)
    hidden = (act * up).astype(low)
    up_factor = act.astype(low)
    gate_factor = (slope * up).astype(low)
    ffn_out = place.scatter_tokens(dot(hidden, down_mat, 1, 0))
    block_output = (middle + rms_norm(ffn_out, norm_gains[3])).astype(low).reshape(tokens.shape)

    grad_rows = cotangent.astype(full).reshape(groups * length, width)
    unused, pull_post = jax.vjp(rms_norm, ffn_out, norm_gains[3])
    ffn_grad, gain_three = pull_post(grad_rows)
    ffn_all = place.gather_tokens(ffn_grad.astype(low))
    down_part = dot(hidden, ffn_all, 0, 0).astype(low)
    hidden_grad = dot(ffn_all, down_mat, 1, 1)
    gate_low = (hidden_grad * gate_factor.astype(full)).astype(low)
    up_low = (hidden_grad * up_factor.astype(full)).astype(low)
    gate_part = dot(gate_low, normed_all, 0, 0).astype(low)
    up_part = dot(up_low, normed_all, 0, 0).astype(low)
    normed_ffn_grad = place.scatter_tokens(dot(gate_low, gate_mat, 1, 0) + dot(up_low, up_mat, 1, 0))

    down_sum = place.scatter_down(down_part.reshape(-1, unit, width))
    gate_up_sum = place.sum_pairs(
        place.scatter_chips(jnp.concatenate([gate_part, up_part], 0).reshape(-1, unit, width))
    )
    other = place.swap_rep(gate_up_sum)
    gate_up_sum = jnp.where(
        par == 0, jnp.stack([gate_up_sum, other]), jnp.stack([other, gate_up_sum])
    ).reshape(2 * unit, width)

    unused, pull_pre = jax.vjp(rms_norm, middle, norm_gains[2])
    middle_part, gain_two = pull_pre(normed_ffn_grad)
    middle_grad = grad_rows + middle_part
    unused, pull_attn = jax.vjp(rms_norm, attn_out, norm_gains[1])
    attn_grad, gain_one = pull_attn(middle_grad)
    attn_low = attn_grad.astype(low)
    out_part = dot(context, attn_low, 0, 0)
    context_grad = dot(attn_low, out_mat, 1, 1).astype(low).reshape(groups, length, -1)
    head_grads = jax.vmap(attend_back)(context_grad, probs, query_low, key_low, value_low)
    unused, pull_heads = jax.vjp(
        lambda rows, gains: jax.vmap(split_heads, (0, None, 0, 0))(rows, gains, cosine, sine_part),
        qkv,
        head_gains,
    )
    qkv_grad, head_grad = pull_heads(head_grads)
    qkv_low = qkv_grad.astype(low).reshape(groups * length, -1)
    qkv_part = dot(qkv_low, normed, 0, 0)
    normed_grad = dot(qkv_low, qkv_mat, 1, 0)
    unused, pull_first = jax.vjp(rms_norm, block_in, norm_gains[0])
    first_part, gain_zero = pull_first(normed_grad)
    input_grad = (middle_grad + first_part).reshape(tokens.shape)

    norm_grad = jnp.stack([gain_zero, gain_one, gain_two, gain_three])
    norm_w, head_w = width // place.shards, HD // place.shards
    gains = jnp.concatenate(
        [
            norm_grad.reshape(4, place.shards, norm_w).transpose(1, 0, 2).reshape(place.shards, -1),
            head_grad.reshape(2, place.shards, head_w).transpose(1, 0, 2).reshape(place.shards, -1),
        ],
        1,
    )
    gains = jnp.pad(gains[:, None, :], ((0, 0), (0, PAD - 1), (0, width - gains.shape[1])))
    attn_part = jnp.concatenate(
        [qkv_part.reshape(place.shards, qw, width), out_part.reshape(place.shards, ow, width), gains], 1
    ).astype(low)
    attn_part = attn_part.reshape((place.chips, 2) + attn_part.shape[1:])
    away = lax.dynamic_index_in_dim(attn_part, 1 - core, 1, keepdims=False)
    mine = lax.dynamic_index_in_dim(attn_part, core, 1, keepdims=False)
    attn_part = (mine.astype(full) + place.swap_core(away).astype(full)).astype(low)
    attn_sum = place.sum_pairs(place.scatter_chips(attn_part))
    attn_sum = attn_sum.astype(full) + place.swap_rep(attn_sum).astype(full)
    qkv_sum = attn_sum[:qw].T
    out_sum = attn_sum[qw : qw + ow]
    gains = attn_sum[qw + ow]
    norm_gain_grad = gains[: 4 * norm_w].reshape(4, norm_w)
    head_gain_grad = gains[4 * norm_w : 4 * norm_w + 2 * head_w].reshape(2, head_w)
    gate_up_grad = gate_up_sum.astype(full).T
    down_grad = down_sum.astype(full)

    total_tokens = groups * length * place.reps * place.shards
    scale = float(total_tokens) ** (-0.5)
    fresh, new_stats = [], []
    for at, (grad, weight, by_column) in enumerate(
        (
            (qkv_sum, qkv_weight, True),
            (out_sum, out_weight, False),
            (gate_up_grad, gate_up_weight, True),
            (down_grad, down_weight, False),
        )
    ):
        left, right, left_root, right_root = stats[4 * at : 4 * at + 4]
        cut = column_blocks if by_column else row_blocks
        sizes = (left.shape[-1], right.shape[-1])
        blocks, new_left, new_right = refresh(
            cut(grad * scale, *sizes), cut(weight, *sizes), left, right, left_root, right_root, decay[at], rate[at]
        )
        fresh.append(column_full(blocks) if by_column else row_full(blocks))
        new_stats += [new_left, new_right]
    return (
        block_output,
        input_grad,
        norm_gain_grad,
        head_gain_grad,
        qkv_sum,
        out_sum,
        gate_up_grad,
        down_grad,
        *fresh,
        *new_stats,
    )


def solution(mesh):
    place = Place(mesh)
    tokens3, rows2 = P(AXES, None, None), P("shard", None)
    columns2, blocks4 = P(None, "shard"), P("shard", None, None, None)

    def run(*args):
        return per_device(place, *args)

    return jax.shard_map(
        run,
        mesh=mesh,
        in_specs=(tokens3, tokens3, P(AXES, None), P(), P(), columns2, rows2, columns2, rows2)
        + (blocks4,) * 16
        + (P(), P()),
        out_specs=(tokens3, tokens3, columns2, columns2, columns2, rows2, columns2, rows2)
        + (columns2, rows2, columns2, rows2)
        + (blocks4,) * 8,
        check_vma=False,
    )
```

```python
import math

import jax
import jax.numpy as jnp
from jax import lax
from jax.experimental import pallas as pl
from jax.experimental.pallas import tpu as pltpu
from jax.sharding import PartitionSpec as P

HQ = 4
HD = 256
AXES = ("rep", "shard")
PAD = 16
MESH = pl.DeviceIdType.MESH

epsilon = 1e-06
rope_base = 1000000.0
low = jnp.bfloat16
full = jnp.float32


def dot(a, b, ca, cb):
    return lax.dot_general(a, b, (((ca,), (cb,)), ((), ())), preferred_element_type=full)


class Place:
    def __init__(self, mesh):
        self.reps = mesh.shape["rep"]
        self.shards = mesh.shape["shard"]
        self.chips = self.shards // 2
        self.outer = min(4, self.chips)
        self.inner = self.chips // self.outer
        self.direct = self.reps == 2 and self.inner == 2

    def here(self):
        r, i = lax.axis_index("rep"), lax.axis_index("shard")
        chip = i // 2
        return r % 2, chip // self.inner, chip % self.inner, i % 2

    def send(self, value, where):
        pairs = []
        for r in range(self.reps):
            for i in range(self.shards):
                o, n, c = i // 2 // self.inner, i // 2 % self.inner, i % 2
                to = where(r, o, n, c)
                if to is not None:
                    r2, o2, n2, c2 = to
                    pairs.append((r * self.shards + i, r2 * self.shards + (o2 * self.inner + n2) * 2 + c2))
        return lax.ppermute(value, AXES, pairs)

    def swap_rep(self, value):
        return self.send(value, lambda r, o, n, c: (r ^ 1, o, n, c))

    def swap_core(self, value):
        return self.send(value, lambda r, o, n, c: (r, o, n, 1 - c))

    def line(self, value, size, move, index):
        up, down = [], []
        send_up = send_down = value
        for k in range(size - 1):
            send_up = move(send_up, 1)
            send_down = move(send_down, -1)
            up.append(send_up)
            down.append(send_down)
        window = jnp.stack(up[::-1] + [value] + down)
        return lax.dynamic_slice_in_dim(window, size - 1 - index, size, 0)

    def move_outer(self, value, by, keep=None):
        def where(r, o, n, c):
            if keep is not None and not keep(n, c):
                return None
            return (r, o + by, n, c) if 0 <= o + by < self.outer else None

        return self.send(value, where)

    def move_inner(self, value, by, keep=None):
        def where(r, o, n, c):
            if keep is not None and not keep(n, c):
                return None
            return (r, o, n + by, c) if 0 <= n + by < self.inner else None

        return self.send(value, where)

    def gather_outer(self, value, keep=None):
        o = self.here()[1]
        return self.line(value, self.outer, lambda v, by: self.move_outer(v, by, keep), o)

    def gather_chips(self, value):
        n = self.here()[2]
        columns = self.gather_outer(value)
        if self.inner == 2:
            other = self.send(columns, lambda r, o, n, c: (r, o, 1 - n, c))
            both = jnp.where(n == 0, jnp.stack([columns, other], 1), jnp.stack([other, columns], 1))
        else:
            both = jnp.swapaxes(self.line(columns, self.inner, self.move_inner, n), 0, 1)
        return both.reshape((self.chips,) + value.shape)

    def scatter_line(self, parts, size, move, index):
        zeros = jnp.zeros_like(parts[:1])
        padded = jnp.concatenate([zeros] * (size - 1) + [parts] + [zeros] * (size - 1), 0)

        def part(offset):
            return lax.dynamic_index_in_dim(padded, index + offset + size - 1, 0, keepdims=False)

        sums = []
        for way in (1, -1):
            got = None
            for k in range(size - 1, 0, -1):
                mine = part(way * k)
                if got is not None:
                    mine = (mine.astype(full) + got.astype(full)).astype(low)
                got = move(mine, way)
            sums.append(got)
        return (part(0).astype(full) + sums[0].astype(full) + sums[1].astype(full)).astype(low)

    def scatter_outer(self, parts, keep=None):
        o = self.here()[1]
        return self.scatter_line(parts, self.outer, lambda v, by: self.move_outer(v, by, keep), o)

    def scatter_chips(self, parts):
        n = self.here()[2]
        parts = parts.reshape((self.outer, self.inner) + parts.shape[1:])
        if self.inner == 2:
            away = lax.dynamic_index_in_dim(parts, 1 - n, 1, keepdims=False)
            mine = lax.dynamic_index_in_dim(parts, n, 1, keepdims=False)
            got = self.send(away, lambda r, o, n, c: (r, o, 1 - n, c))
            column = (mine.astype(full) + got.astype(full)).astype(low)
        else:
            column = self.scatter_line(jnp.swapaxes(parts, 0, 1), self.inner, self.move_inner, n)
        return self.scatter_outer(column)

    def gather_down(self, block):
        par, o, n, c = self.here()
        other = self.swap_core(block)
        mine = jnp.where(par == c, block, other)
        if self.inner == 2:
            keep = lambda n, c: n == c
            column = self.gather_outer(mine, keep)
            got = self.send(column, lambda r, o, n, c: (r, o, 1 - n, c) if n == c else None)
            return jnp.where(n == c, column, got)
        both = self.gather_chips(mine)
        both = both.reshape((self.chips // 2, 2) + block.shape)
        return lax.dynamic_index_in_dim(both, c, 1, keepdims=False)

    def scatter_down(self, parts):
        par, o, n, c = self.here()
        if self.inner == 2:
            keep = lambda n, c: n == c
            got = self.send(parts, lambda r, o, n, c: (r, o, 1 - n, c) if n != c else None)
            column = (parts.astype(full) + got.astype(full)).astype(low)
            own = self.scatter_outer(column, keep)
        else:
            zeros = jnp.zeros_like(parts)
            both = jnp.where(c == 0, jnp.stack([parts, zeros], 1), jnp.stack([zeros, parts], 1))
            own = self.scatter_chips(both.reshape((self.chips,) + parts.shape[1:]))
        own = self.sum_pairs(own)
        far = self.send(own, lambda r, o, n, c: (r ^ 1, o, n, r % 2) if c == n % 2 else None)
        near = self.send(own, lambda r, o, n, c: (r, o, n, r % 2) if c == n % 2 and c != r % 2 else None)
        return jnp.where(c != par, far, jnp.where(c == n % 2, own, near))

    def sum_pairs(self, value):
        if self.reps == 2:
            return value
        groups = [list(range(k, self.reps, 2)) for k in range(2)]
        return lax.psum(value, "rep", axis_index_groups=groups)

    def gather_tokens(self, rows):
        two = jnp.concatenate([rows, self.swap_rep(rows)], 0)
        return jnp.concatenate([two, self.swap_core(two)], 0)

    def scatter_tokens(self, rows):
        half, quarter = rows.shape[0] // 2, rows.shape[0] // 4
        two = rows[:half] + self.swap_core(rows[half:].astype(low)).astype(full)
        return two[:quarter] + self.swap_rep(two[quarter:].astype(low)).astype(full)


class Net:
    def __init__(self, line):
        self.line = line
        r, i = lax.axis_index("rep"), lax.axis_index("shard")
        z, x, c = i // 4, i // 2 % 2, i % 2
        self.r, self.z, self.x, self.c = r, z, x, c

        def at(r, z, x, c):
            return (r, (z * 2 + x) * 2 + c)

        self.up, self.down = at(r, z + 1, x, c), at(r, z - 1, x, c)
        self.across, self.mate, self.diagonal = at(r, z, 1 - x, c), at(r, z, x, 1 - c), at(r, z, 1 - x, 1 - c)
        self.twin, self.twin_mate = at(1 - r, z, x, c), at(1 - r, z, x, 1 - c)
        self.has_up, self.has_down = z < line - 1, z > 0

    def greet(self, others):
        barrier = pltpu.get_barrier_semaphore()

        def signal(to):
            pl.semaphore_signal(barrier, inc=1, device_id=to, device_id_type=MESH)

        pl.when(self.has_up)(lambda: signal(self.up))
        pl.when(self.has_down)(lambda: signal(self.down))
        for to in others:
            signal(to)
        both = self.has_up & self.has_down
        pl.when(both)(lambda: pl.semaphore_wait(barrier, len(others) + 2))
        pl.when(jnp.logical_not(both))(lambda: pl.semaphore_wait(barrier, len(others) + 1))


def put(source, target, send, recv, to):
    return pltpu.make_async_remote_copy(
        src_ref=source, dst_ref=target, send_sem=send, recv_sem=recv, device_id=to, device_id_type=MESH
    )


def gather_weights(place, attn_own, gate_up_own, down_own, qw):
    line, width, unit = place.outer, attn_own.shape[1], down_own.shape[0]
    ow = attn_own.shape[0] - qw
    cut = (unit // 2 + 15) // 16 * 16

    def kernel(attn, gate_up, down, q_all, o_all, g_all, d_all, ts, tr, gs, gr, ds, dr, ls):
        net = Net(line)
        r, z, x, c = net.r, net.z, net.x, net.c
        home, mine = c == x, c == r

        def attn_refs(zz, xx, cc):
            i = (zz * 2 + xx) * 2 + cc
            return [q_all.at[pl.ds(i * qw, qw)], o_all.at[pl.ds(i * ow, ow)]]

        def ways(zz):
            return ((0, net.has_up & (zz <= z), net.up), (1, net.has_down & (zz >= z), net.down))

        def attn_fan(zz, act, own=False):
            for part, ref in enumerate(attn_refs(zz, x, c)):
                source = attn.at[pl.ds(part * qw, (qw, ow)[part])] if own else ref
                for kind, when, to in ways(zz):
                    pl.when(when)(lambda: act(put(source, ref, ts.at[kind, zz, part], tr.at[0, zz, part], to)))
                act(put(source, ref, ts.at[2, zz, part], tr.at[1, zz, part], net.across))
                act(put(source, ref, ts.at[3, zz, part], tr.at[2, zz, part], net.mate))

        def attn_pass(zz, act):
            for part, ref in enumerate(attn_refs(zz, 1 - x, c)):
                act(put(ref, ref, ts.at[4, zz, part], tr.at[3, zz, part], net.mate))

        def attn_wait(zz, kind):
            xx, cc = (x, 1 - x, x, 1 - x)[kind], (c, c, 1 - c, 1 - c)[kind]
            for part, ref in enumerate(attn_refs(zz, xx, cc)):
                put(ref, ref, ts.at[0, zz, part], tr.at[kind, zz, part], net.mate).wait_recv()

        def gate_fan(zz, act, own=False):
            ref = g_all.at[zz * 2 + x]
            source = gate_up if own else ref
            for kind, when, to in ways(zz):
                pl.when(when)(lambda: act(put(source, ref, gs.at[kind, zz], gr.at[0, zz], to)))
            act(put(source, ref, gs.at[2, zz], gr.at[1, zz], net.across))

        def gate_wait(zz, kind):
            ref = g_all.at[zz * 2 + (x, 1 - x)[kind]]
            put(ref, ref, gs.at[0, zz], gr.at[kind, zz], net.mate).wait_recv()

        def down_refs(zz):
            return [d_all.at[zz, pl.ds(0, cut)], d_all.at[zz, pl.ds(cut, unit - cut)]]

        def down_first(act):
            first, second = down_refs(z)
            source = [down.at[pl.ds(0, cut)], down.at[pl.ds(cut, unit - cut)]]

            @pl.when(jnp.logical_not(home))
            def _():
                act(put(source[0], first, ds.at[3, 0, 0], dr.at[0, z, 0], net.mate))
                act(put(source[1], second, ds.at[3, 0, 1], dr.at[0, z, 1], net.mate))
                act(put(source[1], second, ds.at[3, 1, 1], dr.at[0, z, 1], net.diagonal))

            @pl.when(home)
            def _():
                act(put(source[1], second, ds.at[3, 1, 1], dr.at[0, z, 1], net.across))

        def down_fan(zz, act):
            first, second = down_refs(zz)
            for kind, when, to in ways(zz):
                pl.when(when & home)(lambda: act(put(first, first, ds.at[kind, zz, 0], dr.at[0, zz, 0], to)))
                pl.when(when)(lambda: act(put(second, second, ds.at[kind, zz, 1], dr.at[0, zz, 1], to)))
            pl.when(home)(lambda: act(put(first, first, ds.at[2, zz, 0], dr.at[1, zz, 0], net.across)))

        def down_wait(zz, part, kind):
            ref = down_refs(zz)[part]
            put(ref, ref, ds.at[0, zz, part], dr.at[kind, zz, part], net.mate).wait_recv()

        def from_line(k, act):
            for way in (-1, 1):
                zz = z + way * k
                pl.when((zz >= 0) & (zz < line))(lambda: act(zz))

        start, done = (lambda copy: copy.start()), (lambda copy: copy.wait_send())
        net.greet((net.across, net.mate, net.diagonal))
        own_q, own_o = attn_refs(z, x, c)
        local = [
            pltpu.make_async_copy(attn.at[pl.ds(0, qw)], own_q, ls.at[0]),
            pltpu.make_async_copy(attn.at[pl.ds(qw, ow)], own_o, ls.at[1]),
            pltpu.make_async_copy(gate_up, g_all.at[z * 2 + x], ls.at[2]),
        ]
        attn_fan(z, start, True)
        for copy in local:
            copy.start()
        gate_fan(z, start, True)
        keep = pltpu.make_async_copy(down, d_all.at[z], ls.at[3])
        pl.when(mine & home)(lambda: keep.start())

        def attn_on(zz):
            attn_wait(zz, 0)
            attn_fan(zz, start)

        def gate_on(zz):
            gate_wait(zz, 0)
            gate_fan(zz, start)

        def pass_on(zz):
            attn_wait(zz, 1)
            attn_pass(zz, start)

        def down_on(zz):
            pl.when(home)(lambda: down_wait(zz, 0, 0))
            down_wait(zz, 1, 0)
            down_fan(zz, start)

        from_line(1, attn_on)
        pass_on(z)
        from_line(1, gate_on)
        from_line(2, attn_on)
        from_line(1, pass_on)
        from_line(3, attn_on)
        from_line(2, pass_on)
        pl.when(mine)(lambda: down_first(start))
        from_line(2, gate_on)
        pl.when(mine & home)(lambda: keep.wait())
        pl.when(home & jnp.logical_not(mine))(lambda: down_wait(z, 0, 0))
        pl.when(jnp.logical_not(mine & home))(lambda: down_wait(z, 1, 0))
        down_fan(z, start)
        from_line(3, pass_on)
        from_line(3, gate_on)
        for k in range(1, line):
            from_line(k, down_on)
        for zz in range(line):
            attn_wait(zz, 2)
            attn_wait(zz, 3)
            gate_wait(zz, 1)
            pl.when(jnp.logical_not(home))(lambda: down_wait(zz, 0, 1))
        for copy in local:
            copy.wait()
        for zz in range(line):
            attn_fan(zz, done)
            attn_pass(zz, done)
            gate_fan(zz, done)
            down_fan(zz, done)
        pl.when(mine)(lambda: down_first(done))

    anywhere = pl.BlockSpec(memory_space=pl.ANY)
    sems = pltpu.SemaphoreType.DMA
    return pl.pallas_call(
        kernel,
        in_specs=[anywhere] * 3,
        out_specs=[anywhere] * 4,
        out_shape=[
            jax.ShapeDtypeStruct(shape, low)
            for shape in (
                (place.shards * qw, width),
                (place.shards * ow, width),
                (place.chips, unit, width),
                (line, unit, width),
            )
        ],
        scratch_shapes=[
            sems((5, line, 2)),
            sems((4, line, 2)),
            sems((3, line)),
            sems((2, line)),
            sems((4, line, 2)),
            sems((2, line, 2)),
            sems((4,)),
        ],
        compiler_params=pltpu.CompilerParams(collective_id=1, has_side_effects=True),
    )(attn_own, gate_up_own, down_own)


def rms_norm(values, gains):
    return values * lax.rsqrt(jnp.mean(values * values, axis=-1, keepdims=True) + epsilon) * gains


def positions(segment_ids):
    length = segment_ids.shape[0]
    places = jnp.arange(length, dtype=jnp.int32)
    prompt = jnp.sum((segment_ids == 0).astype(jnp.int32))
    before = jnp.sum((segment_ids[None, :] < segment_ids[:, None]).astype(jnp.int32), axis=1)
    return jnp.where(segment_ids == 0, places, prompt + places - before)


def rope_tables(segment_ids):
    half = HD // 2
    spots = positions(segment_ids).astype(full)
    freqs = jnp.exp(jnp.arange(half, dtype=full) * (-2.0 * math.log(rope_base) / HD))
    angles = spots[:, None] * freqs[None, :]
    return (jnp.cos(angles), jnp.sin(angles))


def rotate(values, cosine, sine_part):
    half = values.shape[-1] // 2
    former = values[..., :half]
    latter = values[..., half:]
    return jnp.concatenate(
        [former * cosine - latter * sine_part, latter * cosine + former * sine_part], axis=-1
    )


def allowed_pairs(segment_ids):
    length = segment_ids.shape[0]
    places = jnp.arange(length, dtype=jnp.int32)
    causal = places[:, None] >= places[None, :]
    shared = (segment_ids[None, :] == 0) | (segment_ids[None, :] == segment_ids[:, None])
    return causal & shared


def split_heads(qkv, head_gains, cosine, sine_part):
    length = qkv.shape[0]
    query_rows = qkv[:, : HQ * HD].reshape(length, HQ, HD)
    key_rows = qkv[:, HQ * HD : (HQ + 1) * HD]
    value_rows = qkv[:, (HQ + 1) * HD :]
    query_rows = rotate(
        rms_norm(query_rows, head_gains[0]), cosine[:, None, :], sine_part[:, None, :]
    ) * HD ** (-0.5)
    key_rows = rotate(rms_norm(key_rows, head_gains[1]), cosine, sine_part)
    return (query_rows, key_rows, value_rows)


def attend(query_low, key_low, value_low, allowed):
    scores = jnp.einsum("thd,sd->hts", query_low, key_low, preferred_element_type=full)
    scores = jnp.where(allowed[None], scores, -1000000000.0)
    exponent = jnp.exp(scores - jnp.max(scores, axis=-1, keepdims=True))
    probs = exponent / jnp.sum(exponent, axis=-1, keepdims=True)
    context = jnp.einsum("hts,sd->thd", probs.astype(low), value_low, preferred_element_type=full)
    return probs, context.reshape(context.shape[0], HQ * HD).astype(low)


def attend_back(context_grad, probs, query_low, key_low, value_low):
    context_grad = context_grad.reshape(context_grad.shape[0], HQ, HD)
    prob_grad = jnp.einsum("thd,sd->hts", context_grad, value_low, preferred_element_type=full)
    row_dot = jnp.sum(prob_grad * probs, axis=-1, keepdims=True)
    score_grad = (probs * (prob_grad - row_dot)).astype(low)
    query_grad = jnp.einsum("hts,sd->thd", score_grad, key_low, preferred_element_type=full)
    key_grad = jnp.einsum("hts,thd->sd", score_grad, query_low, preferred_element_type=full)
    value_grad = jnp.einsum("hts,thd->sd", probs.astype(low), context_grad, preferred_element_type=full)
    return query_grad, key_grad, value_grad


def gelu_parts(gate):
    c = math.sqrt(2.0 / math.pi)
    t = jnp.tanh(c * (gate + 0.044715 * gate * gate * gate))
    cdf = 0.5 * (1.0 + t)
    slope = cdf + 0.5 * gate * (1.0 - t * t) * (c * (1.0 + 3.0 * 0.044715 * gate * gate))
    return gate * cdf, slope


def refresh(grads, weight, left_stat, right_stat, left_root, right_root, rates, by_column):
    strips, size, width = grads.shape
    count = left_stat.shape[1]
    rb = width // count

    def kernel(rates_ref, g_ref, w_ref, l_ref, r_ref, lr_ref, rr_ref, g_out, w_out, l_out, r_out):
        decay, rate, scale = rates_ref[0], rates_ref[1], rates_ref[2]
        whole, steps = [], []
        for s in range(strips):
            grad = g_ref[s].astype(full)
            scaled = (grad * scale).astype(low)
            wide = dot(scaled, scaled, 0, 0)
            tall = dot(scaled, scaled, 1, 1)
            left, right = (wide, tall) if by_column else (tall, wide)
            l_out[s, 0] = decay * l_ref[s, 0] + (1.0 - decay) * left
            r_out[s, 0] = decay * r_ref[s, 0] + (1.0 - decay) * right
            first, second = (rr_ref, lr_ref) if by_column else (lr_ref, rr_ref)
            part = dot(first[s, 0].astype(low), scaled, 1, 0).astype(low)
            whole.append(grad)
            steps.append(dot(part, second[s, 0].astype(low), 1, 0))
        grad, step = jnp.concatenate(whole, 0), jnp.concatenate(steps, 0)
        g_out[...] = grad
        w_out[...] = w_ref[...] - rate * step

    flat = pl.BlockSpec((strips * size, rb), lambda i: (0, i))

    def stat(a):
        return pl.BlockSpec((strips, 1) + a.shape[2:], lambda i: (0, i, 0, 0))

    return pl.pallas_call(
        kernel,
        grid=(count,),
        in_specs=[
            pl.BlockSpec(memory_space=pltpu.SMEM),
            pl.BlockSpec((strips, size, rb), lambda i: (0, 0, i)),
            flat,
            stat(left_stat),
            stat(right_stat),
            stat(left_root),
            stat(right_root),
        ],
        out_specs=[flat, flat, stat(left_stat), stat(right_stat)],
        out_shape=[jax.ShapeDtypeStruct(a.shape, full) for a in (weight, weight, left_stat, right_stat)],
        compiler_params=pltpu.CompilerParams(vmem_limit_bytes=48 * 2**20),
        cost_estimate=pl.CostEstimate(
            flops=4 * strips * size * width * (size + rb),
            bytes_accessed=12 * (weight.size + left_stat.size + right_stat.size) + 2 * grads.size,
            transcendentals=0,
        ),
    )(rates, grads, weight, left_stat, right_stat, left_root, right_root)


def per_device(place, tokens, cotangent, segments, norm_gains, head_gains, *rest):
    qkv_weight, out_weight, gate_up_weight, down_weight = rest[:4]
    stats = rest[4:20]
    decay, rate = rest[20:]
    groups, length, width = tokens.shape
    par, outer, inner, core = place.here()
    qw, ow = qkv_weight.shape[1], out_weight.shape[0]
    unit = down_weight.shape[0]

    attn_own = jnp.concatenate([qkv_weight.T, out_weight], 0).astype(low)
    gate_up_own = lax.dynamic_index_in_dim(
        gate_up_weight.T.astype(low).reshape(2, unit, width), par, 0, keepdims=False
    )
    down_own = down_weight.astype(low)
    if place.direct:
        qkv_mat, out_mat, gate_up_all, down_mat = gather_weights(place, attn_own, gate_up_own, down_own, qw)
    else:
        both = place.gather_chips(attn_own)
        mate = place.swap_core(both)
        both = jnp.where(core == 0, jnp.stack([both, mate], 1), jnp.stack([mate, both], 1))
        qkv_mat = both[:, :, :qw].reshape(place.shards * qw, width)
        out_mat = both[:, :, qw:].reshape(place.shards * ow, width)
        gate_up_all = place.gather_chips(gate_up_own)
        down_mat = place.gather_down(down_own)
    hidden_count = place.chips // 2 * unit
    gate_mat = gate_up_all[: place.chips // 2].reshape(hidden_count, width)
    up_mat = gate_up_all[place.chips // 2 :].reshape(hidden_count, width)
    down_mat = down_mat.reshape(hidden_count, width)

    block_in = tokens.astype(full).reshape(groups * length, width)
    cosine, sine_part = jax.vmap(rope_tables)(segments)
    allowed = jax.vmap(allowed_pairs)(segments)
    normed = rms_norm(block_in, norm_gains[0]).astype(low)
    qkv = dot(normed, qkv_mat, 1, 1).reshape(groups, length, -1)
    query_rows, key_rows, value_rows = jax.vmap(split_heads, (0, None, 0, 0))(
        qkv, head_gains, cosine, sine_part
    )
    query_low, key_low, value_low = query_rows.astype(low), key_rows.astype(low), value_rows.astype(low)
    probs, context = jax.vmap(attend)(query_low, key_low, value_low, allowed)
    context = context.reshape(groups * length, HQ * HD)
    attn_out = dot(context, out_mat, 1, 0)
    middle = block_in + rms_norm(attn_out, norm_gains[1])
    normed_ffn = rms_norm(middle, norm_gains[2]).astype(low)
    normed_all = place.gather_tokens(normed_ffn)
    gate = dot(normed_all, gate_mat, 1, 1)
    up = dot(normed_all, up_mat, 1, 1)
    act, slope = gelu_parts(gate)
    hidden = (act * up).astype(low)
    up_factor = act.astype(low)
    gate_factor = (slope * up).astype(low)
    ffn_out = place.scatter_tokens(dot(hidden, down_mat, 1, 0))
    block_output = (middle + rms_norm(ffn_out, norm_gains[3])).astype(low).reshape(tokens.shape)

    grad_rows = cotangent.astype(full).reshape(groups * length, width)
    unused, pull_post = jax.vjp(rms_norm, ffn_out, norm_gains[3])
    ffn_grad, gain_three = pull_post(grad_rows)
    ffn_all = place.gather_tokens(ffn_grad.astype(low))
    down_part = dot(hidden, ffn_all, 0, 0).astype(low)
    hidden_grad = dot(ffn_all, down_mat, 1, 1)
    gate_low = (hidden_grad * gate_factor.astype(full)).astype(low)
    up_low = (hidden_grad * up_factor.astype(full)).astype(low)
    gate_part = dot(gate_low, normed_all, 0, 0).astype(low)
    up_part = dot(up_low, normed_all, 0, 0).astype(low)
    normed_ffn_grad = place.scatter_tokens(dot(gate_low, gate_mat, 1, 0) + dot(up_low, up_mat, 1, 0))

    down_sum = place.scatter_down(down_part.reshape(-1, unit, width))
    gate_up_sum = place.sum_pairs(
        place.scatter_chips(jnp.concatenate([gate_part, up_part], 0).reshape(-1, unit, width))
    )
    other = place.swap_rep(gate_up_sum)
    gate_up_sum = jnp.where(
        par == 0, jnp.stack([gate_up_sum, other]), jnp.stack([other, gate_up_sum])
    ).reshape(2 * unit, width)

    unused, pull_pre = jax.vjp(rms_norm, middle, norm_gains[2])
    middle_part, gain_two = pull_pre(normed_ffn_grad)
    middle_grad = grad_rows + middle_part
    unused, pull_attn = jax.vjp(rms_norm, attn_out, norm_gains[1])
    attn_grad, gain_one = pull_attn(middle_grad)
    attn_low = attn_grad.astype(low)
    out_part = dot(context, attn_low, 0, 0)
    context_grad = dot(attn_low, out_mat, 1, 1).astype(low).reshape(groups, length, -1)
    head_grads = jax.vmap(attend_back)(context_grad, probs, query_low, key_low, value_low)
    unused, pull_heads = jax.vjp(
        lambda rows, gains: jax.vmap(split_heads, (0, None, 0, 0))(rows, gains, cosine, sine_part),
        qkv,
        head_gains,
    )
    qkv_grad, head_grad = pull_heads(head_grads)
    qkv_low = qkv_grad.astype(low).reshape(groups * length, -1)
    qkv_part = dot(qkv_low, normed, 0, 0)
    normed_grad = dot(qkv_low, qkv_mat, 1, 0)
    unused, pull_first = jax.vjp(rms_norm, block_in, norm_gains[0])
    first_part, gain_zero = pull_first(normed_grad)
    input_grad = (middle_grad + first_part).reshape(tokens.shape)

    norm_grad = jnp.stack([gain_zero, gain_one, gain_two, gain_three])
    norm_w, head_w = width // place.shards, HD // place.shards
    gains = jnp.concatenate(
        [
            norm_grad.reshape(4, place.shards, norm_w).transpose(1, 0, 2).reshape(place.shards, -1),
            head_grad.reshape(2, place.shards, head_w).transpose(1, 0, 2).reshape(place.shards, -1),
        ],
        1,
    )
    gains = jnp.pad(gains[:, None, :], ((0, 0), (0, PAD - 1), (0, width - gains.shape[1])))
    attn_part = jnp.concatenate(
        [qkv_part.reshape(place.shards, qw, width), out_part.reshape(place.shards, ow, width), gains], 1
    ).astype(low)
    attn_part = attn_part.reshape((place.chips, 2) + attn_part.shape[1:])
    away = lax.dynamic_index_in_dim(attn_part, 1 - core, 1, keepdims=False)
    mine = lax.dynamic_index_in_dim(attn_part, core, 1, keepdims=False)
    attn_part = (mine.astype(full) + place.swap_core(away).astype(full)).astype(low)
    attn_sum = place.sum_pairs(place.scatter_chips(attn_part))
    attn_sum = attn_sum.astype(full) + place.swap_rep(attn_sum).astype(full)
    gains = attn_sum[qw + ow]
    norm_gain_grad = gains[: 4 * norm_w].reshape(4, norm_w)
    head_gain_grad = gains[4 * norm_w : 4 * norm_w + 2 * head_w].reshape(2, head_w)

    total_tokens = groups * length * place.reps * place.shards
    scale = float(total_tokens) ** (-0.5)
    grads, fresh, new_stats = [], [], []
    for at, (grad, weight, by_column) in enumerate(
        (
            (attn_sum[:qw], qkv_weight, True),
            (attn_sum[qw : qw + ow], out_weight, False),
            (gate_up_sum, gate_up_weight, True),
            (down_sum, down_weight, False),
        )
    ):
        left, right, left_root, right_root = stats[4 * at : 4 * at + 4]
        strips = left.shape[0]
        rates = jnp.stack([decay[at], rate[at], jnp.float32(scale)])
        if by_column:
            weight = weight.T
        grad, weight, left, right = refresh(
            grad.reshape(strips, -1, width), weight, left, right, left_root, right_root, rates, by_column
        )
        if by_column:
            grad, weight = grad.T, weight.T
        grads.append(grad)
        fresh.append(weight)
        new_stats += [left, right]
    return (block_output, input_grad, norm_gain_grad, head_gain_grad, *grads, *fresh, *new_stats)


def solution(mesh):
    place = Place(mesh)
    tokens3, rows2 = P(AXES, None, None), P("shard", None)
    columns2, blocks4 = P(None, "shard"), P("shard", None, None, None)

    def run(*args):
        return per_device(place, *args)

    return jax.shard_map(
        run,
        mesh=mesh,
        in_specs=(tokens3, tokens3, P(AXES, None), P(), P(), columns2, rows2, columns2, rows2)
        + (blocks4,) * 16
        + (P(), P()),
        out_specs=(tokens3, tokens3, columns2, columns2, columns2, rows2, columns2, rows2)
        + (columns2, rows2, columns2, rows2)
        + (blocks4,) * 8,
        check_vma=False,
    )
```
